256 devices in a mesh: seq: 16 (over z_hi, x), tp: 4 (over y), batch: 4 (over z_lo, core).
Axes of the slice: x: 4, y: 4, z: 8 (z_hi: 4, z_lo: 2; z = z_hi * 2 + z_lo), core: 2. Of those that a mesh axis runs over, the one named last changes fastest.
Arguments:
- tokens: bfloat16 [8192, 3072], P(('batch', 'seq')), parts along dimension 0, may hold values from -6 to 6
- tangents: bfloat16 [8192, 3072], P(('batch', 'seq')), parts along dimension 0, may hold values from -6 to 6
- qkv_weight: bfloat16 [3072, 16, 3, 128], P('seq', 'tp'), may hold values from -0.109375 to 0.109375
- out_weight: bfloat16 [3072, 16, 128], P('seq', 'tp'), may hold values from -0.5 to 0.5
- mod_shift: float32 [12288], P('batch'), parts along dimension 0, may hold values from -3 to 3
- mod_scale: float32 [12288], P('batch'), parts along dimension 0, may hold values from -3 to 3
- mod_gate: float32 [12288], P('batch'), parts along dimension 0, may hold values from -8 to 8
- query_gain: float32 [128], replicated, may hold values from 0.5 to 2
- key_gain: float32 [128], replicated, may hold values from 0.5 to 2
Outputs:
- result: bfloat16 [8192, 3072], P(('batch', 'seq'), 'tp'), parts along dimension 0
- result_tangent: bfloat16 [8192, 3072], P(('batch', 'seq'), 'tp'), parts along dimension 0
The draws below stay inside these ranges and needn't reach their ends.
There are 4 independent parts, one for each index of `batch`. The reference program is written for one: setup_inputs(seed, part) draws one part's arguments, and reference() takes and returns one part's arrays. A program takes and returns all parts, laid end to end along the dimension named above; an argument that names none is the same for every part. Nothing has to cross between parts.
All inputs are finite; a program needn't handle non-finite values.
Results may differ from the reference program's by a relative error of at most 0.017.
Values may be sent and summed in bfloat16 or wider, within the bound.
No kernel may reach another device: no remote copies, remote signals or barrier semaphores. Data moves between devices by JAX's collectives and lax.ppermute only.
A program may use at most 64 MiB of HBM per device.

```python
import jax
import jax.numpy as jnp
from jax import lax

D = 3072
HEADS = 16
HD = 128
TOKENS = 2048


def block_levels(key, dims, cuts, low, high):
    gain = 1.0
    for position, shards_of in cuts:
        draws = jax.random.uniform(jax.random.fold_in(jax.random.fold_in(key, 6), position), (shards_of,), jnp.float32, low / len(cuts), high / len(cuts))
        gain = gain * jnp.repeat(jnp.exp(draws), dims[position] // shards_of).reshape((-1,) + (1,) * (len(dims) - 1 - position))
    return gain


def normal_values(stream_key, shape, scale, most, split=(), held_as=jnp.bfloat16):
    values = scale * jax.random.normal(stream_key, shape, jnp.float32)
    if split:
        values = values * block_levels(stream_key, shape, split, -0.22, 0.18)
    return jnp.clip(values, -most, most).astype(held_as)


def setup_inputs(seed: int = 0, part: int = 0) -> dict:
    key_list = jax.random.split(jax.random.key(seed), 10)
    own_keys = jax.random.split(jax.random.fold_in(key_list[9], part), 10)
    tokens = normal_values(own_keys[0], (TOKENS, D), 1.0, 6.0, ((0, 16),))
    tangents = normal_values(own_keys[1], (TOKENS, D), 1.0, 6.0, ((0, 16),))
    qkv_weight = normal_values(key_list[2], (D, HEADS, 3, HD), D ** -0.5, 0.109375, ((0, 16), (1, 4)))
    out_weight = normal_values(key_list[3], (D, HEADS, HD), HD ** -0.5, 0.5, ((0, 16), (1, 4)))
    mod_shift = normal_values(own_keys[4], (D,), 0.5, 3.0, (), jnp.float32)
    mod_scale = normal_values(own_keys[5], (D,), 0.5, 3.0, (), jnp.float32)
    mod_gate = normal_values(own_keys[6], (D,), 2.0, 8.0, (), jnp.float32)
    query_gain = jnp.clip(jax.random.uniform(key_list[7], (HD,), jnp.float32, 0.5, 2.0), 0.5, 2.0)
    key_gain = jnp.clip(jax.random.uniform(key_list[8], (HD,), jnp.float32, 0.5, 2.0), 0.5, 2.0)
    return {"tokens": tokens, "tangents": tangents, "qkv_weight": qkv_weight, "out_weight": out_weight, "mod_shift": mod_shift, "mod_scale": mod_scale, "mod_gate": mod_gate, "query_gain": query_gain, "key_gain": key_gain}


epsilon = 1e-06

def modulate(block_in, mod_shift, mod_scale):
    values = block_in.astype(jnp.float32)
    center = lax.optimization_barrier(jnp.mean(values, axis=-1, keepdims=True))
    spread = lax.optimization_barrier(jnp.mean((values - center) ** 2, axis=-1, keepdims=True))
    return ((values - center) * lax.rsqrt(spread + epsilon) * (1.0 + mod_scale) + mod_shift).astype(jnp.bfloat16)

def finish_heads(proj, query_gain, key_gain):
    queries = proj[:, :, 0]
    keys_part = proj[:, :, 1]
    queries = queries * lax.rsqrt(lax.optimization_barrier(jnp.mean(queries * queries, axis=-1, keepdims=True)) + epsilon) * query_gain
    keys_part = keys_part * lax.rsqrt(lax.optimization_barrier(jnp.mean(keys_part * keys_part, axis=-1, keepdims=True)) + epsilon) * key_gain
    return jnp.stack([queries, keys_part, proj[:, :, 2]], axis=2).astype(jnp.bfloat16)

def attend(queries, keys_part, values):
    inverse = 1.0 / jnp.sqrt(jnp.float32(queries.shape[-1]))
    scores = lax.dot_general(queries, keys_part, (((1,), (1,)), ((), ())), preferred_element_type=jnp.float32) * inverse
    weights = jax.nn.softmax(scores, axis=-1).astype(jnp.bfloat16)
    return jnp.dot(weights, values, preferred_element_type=jnp.float32).astype(jnp.bfloat16)

def reference(tokens, tangents, qkv_weight, out_weight, mod_shift, mod_scale, mod_gate, query_gain, key_gain):

    def block(block_in):
        normed = modulate(block_in, mod_shift, mod_scale)
        proj = jnp.dot(normed, qkv_weight.reshape(D, HEADS * 3 * HD), preferred_element_type=jnp.float32)
        packed = finish_heads(proj.reshape(TOKENS, HEADS, 3, HD), query_gain, key_gain)
        by_head = jnp.moveaxis(packed, 1, 0)

        def one_head(head_data):
            return attend(head_data[:, 0], head_data[:, 1], head_data[:, 2])
        attended = lax.map(one_head, by_head)
        attended = jnp.moveaxis(attended, 0, 1).reshape(TOKENS, HEADS * HD)
        branch = lax.dot_general(attended, out_weight.reshape(D, HEADS * HD), (((1,), (1,)), ((), ())), preferred_element_type=jnp.float32)
        return (block_in.astype(jnp.float32) + mod_gate * branch).astype(jnp.bfloat16)
    result, result_tangent = jax.jvp(block, (tokens,), (tangents,))
    return (result, result_tangent)
```

```python
import functools

import jax
import jax.numpy as jnp
from jax import lax
from jax.experimental import pallas as pl
from jax.experimental.pallas import tpu as pltpu
from jax.sharding import Mesh, PartitionSpec as P

epsilon = 1e-06
MIB = 1 << 20
f32 = jnp.float32
bf16 = jnp.bfloat16


def dot_nt(a, b):
    return lax.dot_general(a, b, (((1,), (1,)), ((), ())), preferred_element_type=f32)


def modulate_kernel(tok_ref, tan_ref, shift_ref, scale_ref, out_ref):
    groups, _, _, width = out_ref.shape
    part = width // groups
    gain = 1.0 + scale_ref[...]
    values = tok_ref[...].astype(f32)
    dots = tan_ref[...].astype(f32)
    center = values - jnp.mean(values, axis=-1, keepdims=True)
    center_dot = dots - jnp.mean(dots, axis=-1, keepdims=True)
    spread = jnp.mean(center * center, axis=-1, keepdims=True)
    spread_dot = 2.0 * jnp.mean(center * center_dot, axis=-1, keepdims=True)
    root = lax.rsqrt(spread + epsilon)
    root_dot = -0.5 * root * root * root * spread_dot
    normed = (center * root * gain + shift_ref[...]).astype(bf16)
    normed_dot = ((center_dot * root + center * root_dot) * gain).astype(bf16)
    for high in range(groups):
        for low in range(groups):
            start = (high * groups + low) * part
            out_ref[low, 0, :, high * part : (high + 1) * part] = normed[:, start : start + part]
            out_ref[low, 1, :, high * part : (high + 1) * part] = normed_dot[:, start : start + part]


def modulate(tokens, tangents, shift, scale):
    rows, width = tokens.shape
    step = 32
    return pl.pallas_call(
        modulate_kernel,
        grid=(rows // step,),
        in_specs=[
            pl.BlockSpec((step, width), lambda i: (i, 0)),
            pl.BlockSpec((step, width), lambda i: (i, 0)),
            pl.BlockSpec((1, width), lambda i: (0, 0)),
            pl.BlockSpec((1, width), lambda i: (0, 0)),
        ],
        out_specs=pl.BlockSpec((4, 2, step, width // 4), lambda i: (0, 0, i, 0)),
        out_shape=jax.ShapeDtypeStruct((4, 2, rows, width // 4), bf16),
        compiler_params=pltpu.CompilerParams(vmem_limit_bytes=16 * MIB),
        cost_estimate=pl.CostEstimate(flops=20 * rows * width, bytes_accessed=8 * rows * width, transcendentals=0),
    )(tokens, tangents, shift.reshape(1, width), scale.reshape(1, width))


def project_kernel(n0_ref, n1_ref, n2_ref, n3_ref, w_ref, gain_ref, out_ref, acc_ref):
    group = pl.program_id(0)

    @pl.when(group == 0)
    def _():
        acc_ref[...] = jnp.zeros_like(acc_ref)

    for r, ref in enumerate((n0_ref, n1_ref, n2_ref, n3_ref)):
        acc_ref[r] += jnp.dot(ref[0], w_ref[0], preferred_element_type=f32)

    @pl.when(group == pl.num_programs(0) - 1)
    def _():
        rows = acc_ref.shape[1] // 2
        for r in range(4):
            for kind in range(3):
                part = acc_ref[r, :rows, kind * 128 : (kind + 1) * 128]
                part_dot = acc_ref[r, rows:, kind * 128 : (kind + 1) * 128]
                if kind < 2:
                    root = lax.rsqrt(jnp.mean(part * part, axis=-1, keepdims=True) + epsilon)
                    root_dot = -root * root * root * jnp.mean(part * part_dot, axis=-1, keepdims=True)
                    gain = gain_ref[kind : kind + 1, :]
                    part, part_dot = part * root * gain, (part_dot * root + part * root_dot) * gain
                place = (4, 0, 2)[kind]
                out_ref[r, place] = part.astype(bf16)
                out_ref[r, place + 1] = part_dot.astype(bf16)


def project(parts, weight, gains):
    groups, rows, depth = parts[0].shape
    cols = weight.shape[2]
    part_spec = pl.BlockSpec((1, rows, depth), lambda q: (q, 0, 0))
    return pl.pallas_call(
        project_kernel,
        grid=(groups,),
        in_specs=[part_spec] * 4
        + [pl.BlockSpec((1, depth, cols), lambda q: (q, 0, 0)), pl.BlockSpec((2, 128), lambda q: (0, 0))],
        out_specs=pl.BlockSpec((4, 6, rows // 2, 128), lambda q: (0, 0, 0, 0)),
        out_shape=jax.ShapeDtypeStruct((4, 6, rows // 2, 128), bf16),
        scratch_shapes=[pltpu.VMEM((4, rows, cols), f32)],
        compiler_params=pltpu.CompilerParams(vmem_limit_bytes=24 * MIB),
        cost_estimate=pl.CostEstimate(
            flops=8 * groups * rows * depth * cols, bytes_accessed=10 * MIB, transcendentals=0
        ),
    )(*parts, weight, gains)


def attend_kernel(counts, *refs):
    kv_refs = refs[: len(counts)]
    q_refs = refs[len(counts) : len(counts) + 4]
    out_ref, q_cat, k_cat, v_cat, e_ref, sd_ref = refs[len(counts) + 4 :]
    rows = 128
    for i, ref in enumerate(q_refs):
        q_cat[i * rows : (i + 1) * rows, :128] = ref[1]
        q_cat[i * rows : (i + 1) * rows, 128:] = ref[0]
    at = 0
    for count, ref in zip(counts, kv_refs):
        for n in range(count):
            k_cat[at : at + rows, :128] = ref[4 * n]
            k_cat[at : at + rows, 128:] = ref[4 * n + 1]
            v_cat[at : at + rows, :128] = ref[4 * n + 2]
            v_cat[at : at + rows, 128:] = ref[4 * n + 3]
            at += rows
    inverse = 128.0 ** -0.5
    chunk = 256
    total_rows = q_cat.shape[0]
    weight_sum = jnp.zeros((total_rows, 128), f32)
    dot_sum = jnp.zeros((total_rows, 128), f32)
    for at in range(0, k_cat.shape[0], chunk):
        keys = k_cat[at : at + chunk, :]
        scores = dot_nt(q_cat[:, 128:], keys[:, :128])
        scores_dot = dot_nt(q_cat[...], keys)
        weights = jnp.exp2(scores * (inverse * 1.4426950408889634))
        e_ref[:, at : at + chunk] = weights
        sd_ref[:, at : at + chunk] = scores_dot
        both = weights * scores_dot
        weight_sum += weights[:, :128] + weights[:, 128:]
        dot_sum += both[:, :128] + both[:, 128:]
    scale = 1.0 / jnp.sum(weight_sum, axis=-1, keepdims=True)
    center = jnp.sum(dot_sum, axis=-1, keepdims=True) * scale
    summed = jnp.zeros((total_rows, 256), f32)
    summed_dot = jnp.zeros((total_rows, 128), f32)
    for at in range(0, k_cat.shape[0], chunk):
        weights = e_ref[:, at : at + chunk]
        weights_dot = (weights * (sd_ref[:, at : at + chunk] - center)).astype(bf16)
        values = v_cat[at : at + chunk, :]
        summed += jnp.dot(weights.astype(bf16), values, preferred_element_type=f32)
        summed_dot += jnp.dot(weights_dot, values[:, :128], preferred_element_type=f32)
    primal = (summed[:, :128] * scale).astype(bf16)
    tangent = ((summed[:, 128:] + summed_dot * inverse) * scale).astype(bf16)
    for i in range(4):
        out_ref[i, 0] = primal[i * rows : (i + 1) * rows]
        out_ref[i, 1] = tangent[i * rows : (i + 1) * rows]


def attend(key_parts, query_parts):
    counts = tuple(part.shape[0] // 4 for part in key_parts)
    keys = 128 * sum(counts)
    return pl.pallas_call(
        functools.partial(attend_kernel, counts),
        out_shape=jax.ShapeDtypeStruct((4, 2, 128, 128), bf16),
        scratch_shapes=[
            pltpu.VMEM((512, 256), bf16),
            pltpu.VMEM((keys, 256), bf16),
            pltpu.VMEM((keys, 256), bf16),
            pltpu.VMEM((512, keys), f32),
            pltpu.VMEM((512, keys), f32),
        ],
        compiler_params=pltpu.CompilerParams(vmem_limit_bytes=32 * MIB),
        cost_estimate=pl.CostEstimate(
            flops=2 * 512 * keys * 128 * 6, bytes_accessed=3 * MIB, transcendentals=512 * keys
        ),
    )(*key_parts, *query_parts)


def finish_kernel(order_ref, h0, h1, h2, h3, w_ref, tok_ref, tan_ref, gate_ref, out_ref, out_dot_ref):
    rows = tok_ref.shape[0]
    total = jnp.zeros((2 * rows, w_ref.shape[1]), f32)
    for m, ref in enumerate((h0, h1, h2, h3)):
        for i in range(4):
            total += dot_nt(ref[i], w_ref[order_ref[4 * m + i]])
    gate = gate_ref[...]
    out_ref[...] = (tok_ref[...].astype(f32) + gate * total[:rows]).astype(bf16)
    out_dot_ref[...] = (tan_ref[...].astype(f32) + gate * total[rows:]).astype(bf16)


def finish(order, parts, weight, tokens, tangents, gate):
    rows, cols = tokens.shape
    step = 256
    part_spec = pl.BlockSpec(parts[0].shape, lambda n, s: (0, 0, 0))
    col_spec = pl.BlockSpec((rows, step), lambda n, s: (0, n))
    return pl.pallas_call(
        finish_kernel,
        grid_spec=pltpu.PrefetchScalarGridSpec(
            num_scalar_prefetch=1,
            grid=(cols // step,),
            in_specs=[part_spec] * 4
            + [
                pl.BlockSpec((16, step, 128), lambda n, s: (0, n, 0)),
                col_spec,
                col_spec,
                pl.BlockSpec((1, step), lambda n, s: (0, n)),
            ],
            out_specs=[col_spec, col_spec],
        ),
        out_shape=[jax.ShapeDtypeStruct((rows, cols), bf16)] * 2,
        compiler_params=pltpu.CompilerParams(vmem_limit_bytes=16 * MIB),
        cost_estimate=pl.CostEstimate(flops=4 * rows * cols * 2048, bytes_accessed=6 * MIB, transcendentals=0),
    )(order, *parts, weight, tokens, tangents, gate)


def from_ahead(array, axis, k):
    if k % 4 == 0:
        return array
    return lax.ppermute(array, axis, [(i, (i - k) % 4) for i in range(4)])


def swap(array, axis):
    return lax.ppermute(array, axis, [(0, 1), (1, 0)])


def pick(array, index, axis=0):
    return lax.dynamic_index_in_dim(array, index, axis, keepdims=False)


def place(pieces, positions):
    out = jnp.zeros((len(pieces),) + pieces[0].shape, pieces[0].dtype)
    for piece, position in zip(pieces, positions):
        out = lax.dynamic_update_index_in_dim(out, piece, position, 0)
    return out


def per_device(tokens, tangents, qkv_weight, out_weight, mod_shift, mod_scale, mod_gate, query_gain, key_gain):
    zh, x, y = (lax.axis_index(name) for name in ("zh", "x", "y"))
    zl, c = lax.axis_index("zl"), lax.axis_index("c")
    clip = 2 * zl + c
    rows, features = tokens.shape
    ahead = lambda base, k: (base + k) % 4

    own_weight = pick(qkv_weight, clip, 1).reshape(qkv_weight.shape[0], 384)
    columns = place([from_ahead(own_weight, "zh", k) for k in range(4)], [ahead(zh, k) for k in range(4)])
    columns = columns.reshape(-1, 384)
    weight = place([from_ahead(columns, "x", k) for k in range(4)], [ahead(x, k) for k in range(4)])

    normed = modulate(tokens, tangents, mod_shift, mod_scale).reshape(4, 2 * rows, features // 4)
    quarter = swap(pick(normed, y), "zl")
    far = [from_ahead(quarter, "y", k) for k in range(4)]
    spots = [ahead(y, k) for k in range(4)]
    far_swapped = place([swap(piece, "c") for piece in far], spots)
    parts = [normed, swap(normed, "c"), place(far, spots), far_swapped]
    packed = project(parts, weight, jnp.stack([query_gain, key_gain]))

    got = []
    for k in range(4):
        block = pick(packed, ahead(zh, k) ^ clip)
        got.append(from_ahead(block, "zh", -k))
    groups = [got[0][:4], jnp.concatenate([got[1][:4], got[3][:4]]), got[2][:4]]
    key_parts = [from_ahead(group, "x", m) for group in groups for m in range(4)]
    attended = attend(key_parts, [part[4:] for part in got])

    heads = []
    for i in range(4):
        piece = pick(attended, (zh - clip - i) % 4).reshape(2 * rows, 128)
        perm = [
            (a * 4 + j, ((j + i) % 4) * 4 + a)
            for a in range(4)
            for j in range(4)
        ]
        heads.append(lax.ppermute(piece, ("zh", "zl", "c"), perm))
    heads = jnp.stack(heads)
    all_heads = [from_ahead(heads, "y", m) for m in range(4)]
    order = jnp.stack([ahead(y, m) * 4 + ahead(zh, -i) for m in range(4) for i in range(4)]).astype(jnp.int32)

    half = jnp.moveaxis(lax.dynamic_slice_in_dim(out_weight, 2 * c, 2, 1), 1, 0)
    half, _ = lax.optimization_barrier((half, packed))
    pieces = []
    for i in range(4):
        perm = [(a * 4 + b, ((b - i) % 4) * 4 + a) for a in range(4) for b in range(4)]
        pieces.append(lax.ppermute(half, ("zh", "y"), perm))
    columns = place(pieces, [ahead(zh, i) for i in range(4)])
    full = jnp.zeros(columns.shape[:2] + (4,) + columns.shape[2:], bf16)
    for m in range(4):
        full = lax.dynamic_update_index_in_dim(full, from_ahead(columns, "x", m), ahead(x, m), 2)
    other = swap(full, "c")
    out_full = jnp.zeros((4, 4) + full.shape[2:], bf16)
    out_full = lax.dynamic_update_slice_in_dim(out_full, full, 2 * c, 1)
    out_full = lax.dynamic_update_slice_in_dim(out_full, other, 2 - 2 * c, 1)
    share = features // 4
    out_full = out_full.reshape(16, share, 128)

    offset = y * share
    tokens_part = lax.dynamic_slice_in_dim(tokens, offset, share, 1)
    tangents_part = lax.dynamic_slice_in_dim(tangents, offset, share, 1)
    gate_part = lax.dynamic_slice_in_dim(mod_gate, offset, share, 0).reshape(1, share)
    result, result_tangent = finish(order, all_heads, out_full, tokens_part, tangents_part, gate_part)
    return (result, result_tangent)


def solution(mesh):
    split = Mesh(mesh.devices.reshape(4, 4, 4, 2, 2), ("zh", "x", "y", "zl", "c"))
    rows = P(("zl", "c", "zh", "x"), None)
    clip = P(("zl", "c"))
    return jax.shard_map(
        per_device,
        mesh=split,
        in_specs=(
            rows,
            rows,
            P(("zh", "x"), "y", None, None),
            P(("zh", "x"), "y", None),
            clip,
            clip,
            clip,
            P(),
            P(),
        ),
        out_specs=(P(("zl", "c", "zh", "x"), "y"), P(("zl", "c", "zh", "x"), "y")),
        check_vma=False,
    )
```

```python
import functools

import jax
import jax.numpy as jnp
from jax import lax
from jax.experimental import pallas as pl
from jax.experimental.pallas import tpu as pltpu
from jax.sharding import Mesh, PartitionSpec as P

epsilon = 1e-06
MIB = 1 << 20
f32 = jnp.float32
bf16 = jnp.bfloat16


def dot_nt(a, b):
    return lax.dot_general(a, b, (((1,), (1,)), ((), ())), preferred_element_type=f32)


def modulate_kernel(y_ref, tok_ref, tan_ref, shift_ref, scale_ref, out_ref, quarter_ref):
    groups, _, _, width = out_ref.shape
    part = width // groups
    gain = 1.0 + scale_ref[...]
    values = tok_ref[...].astype(f32)
    dots = tan_ref[...].astype(f32)
    center = values - jnp.mean(values, axis=-1, keepdims=True)
    center_dot = dots - jnp.mean(dots, axis=-1, keepdims=True)
    spread = jnp.mean(center * center, axis=-1, keepdims=True)
    spread_dot = 2.0 * jnp.mean(center * center_dot, axis=-1, keepdims=True)
    root = lax.rsqrt(spread + epsilon)
    root_dot = -0.5 * root * root * root * spread_dot
    normed = (center * root * gain + shift_ref[...]).astype(bf16)
    normed_dot = ((center_dot * root + center * root_dot) * gain).astype(bf16)
    for high in range(groups):
        for low in range(groups):
            start = (high * groups + low) * part
            out_ref[low, 0, :, high * part : (high + 1) * part] = normed[:, start : start + part]
            out_ref[low, 1, :, high * part : (high + 1) * part] = normed_dot[:, start : start + part]
    quarter_ref[...] = out_ref[y_ref[0]]


def modulate(y, tokens, tangents, shift, scale):
    rows, width = tokens.shape
    step = 32
    token_spec = pl.BlockSpec((step, width), lambda i, s: (i, 0))
    whole_spec = pl.BlockSpec((1, width), lambda i, s: (0, 0))
    return pl.pallas_call(
        modulate_kernel,
        grid_spec=pltpu.PrefetchScalarGridSpec(
            num_scalar_prefetch=1,
            grid=(rows // step,),
            in_specs=[token_spec, token_spec, whole_spec, whole_spec],
            out_specs=[
                pl.BlockSpec((4, 2, step, width // 4), lambda i, s: (0, 0, i, 0)),
                pl.BlockSpec((2, step, width // 4), lambda i, s: (0, i, 0)),
            ],
        ),
        out_shape=[
            jax.ShapeDtypeStruct((4, 2, rows, width // 4), bf16),
            jax.ShapeDtypeStruct((2, rows, width // 4), bf16),
        ],
        compiler_params=pltpu.CompilerParams(vmem_limit_bytes=56 * MIB),
        cost_estimate=pl.CostEstimate(flops=20 * rows * width, bytes_accessed=8 * rows * width, transcendentals=0),
    )(y.reshape(1).astype(jnp.int32), tokens, tangents, shift.reshape(1, width), scale.reshape(1, width))


smem = pl.BlockSpec(memory_space=pltpu.SMEM)
vmem = pl.BlockSpec(memory_space=pltpu.VMEM)


def three_kernel(spot_ref, n0_ref, n1_ref, w0_ref, w1_ref, w3_ref, out_ref):
    x, s = spot_ref[0], spot_ref[1]
    for r, ref in enumerate((n0_ref, n1_ref)):
        total = None
        for n, w_ref in enumerate((w0_ref, w1_ref, w3_ref)):
            term = jnp.dot(ref[(x + (0, s, 4 - s)[n]) % 4], w_ref[...], preferred_element_type=f32)
            total = term if total is None else total + term
        out_ref[r] = total


def project_three(spot, parts, weights):
    shape = (2, parts[0].shape[1], weights[0].shape[1])
    return pl.pallas_call(
        three_kernel,
        in_specs=[smem] + [vmem] * 5,
        out_specs=vmem,
        out_shape=jax.ShapeDtypeStruct(shape, f32),
        compiler_params=pltpu.CompilerParams(vmem_limit_bytes=24 * MIB),
        cost_estimate=pl.CostEstimate(flops=2 * 3 * 768 * 512 * 384, bytes_accessed=6 * MIB, transcendentals=0),
    )(spot, *parts, *weights)


def last_kernel(spot_ref, n0_ref, n1_ref, n2_ref, n3_ref, w_ref, near_ref, far_ref, gain_ref, *refs):
    *out_refs, own_ref, held_ref = refs
    rows = n0_ref.shape[1] // 2
    for r, ref in enumerate((n0_ref, n1_ref, n2_ref, n3_ref)):
        before = near_ref[r] if r < 2 else far_ref[r - 2]
        total = before + jnp.dot(ref[0], w_ref[...], preferred_element_type=f32)
        for kind in range(3):
            part = total[:rows, kind * 128 : (kind + 1) * 128]
            part_dot = total[rows:, kind * 128 : (kind + 1) * 128]
            if kind < 2:
                root = lax.rsqrt(jnp.mean(part * part, axis=-1, keepdims=True) + epsilon)
                root_dot = -root * root * root * jnp.mean(part * part_dot, axis=-1, keepdims=True)
                gain = gain_ref[kind : kind + 1, :]
                part, part_dot = part * root * gain, (part_dot * root + part * root_dot) * gain
            at = (4, 0, 2)[kind]
            held_ref[r, at] = part.astype(bf16)
            held_ref[r, at + 1] = part_dot.astype(bf16)
    for k, ref in enumerate(out_refs):
        ref[...] = held_ref[spot_ref[1 + k], : ref.shape[0]]
    own_ref[...] = held_ref[spot_ref[1], 4:]


def project_last(spot, parts, weight, near, far, gains):
    groups, rows, depth = parts[0].shape
    whole = lambda shape: pl.BlockSpec(shape, lambda n, s: (0,) * len(shape))
    part_spec = pl.BlockSpec((1, rows, depth), lambda n, s: (s[0], 0, 0))
    extra = [weight, near, far, gains]
    shapes = [(4, rows // 2, 128)] + [(6, rows // 2, 128)] * 3 + [(2, rows // 2, 128)]
    return pl.pallas_call(
        last_kernel,
        grid_spec=pltpu.PrefetchScalarGridSpec(
            num_scalar_prefetch=1,
            grid=(1,),
            in_specs=[part_spec] * 4 + [whole(a.shape) for a in extra],
            out_specs=[whole(shape) for shape in shapes],
            scratch_shapes=[pltpu.VMEM((4, 6, rows // 2, 128), bf16)],
        ),
        out_shape=[jax.ShapeDtypeStruct(shape, bf16) for shape in shapes],
        compiler_params=pltpu.CompilerParams(vmem_limit_bytes=24 * MIB),
        cost_estimate=pl.CostEstimate(flops=8 * rows * depth * 384, bytes_accessed=5 * MIB, transcendentals=0),
    )(spot, *parts, *extra)


def attend_kernel(counts, spot_ref, *refs):
    kv_refs = refs[: len(counts)]
    own_refs = refs[len(counts) : len(counts) + 3]
    first_ref, *out_refs, q_cat, k_cat, v_cat, e_ref, sd_ref, held_ref = refs[len(counts) + 3 :]
    rows = 128
    for i, ref in enumerate((first_ref,) + own_refs):
        at = 0 if i == 0 else 4
        q_cat[i * rows : (i + 1) * rows, :128] = ref[at + 1]
        q_cat[i * rows : (i + 1) * rows, 128:] = ref[at]
    at = 0
    for count, ref in zip(counts + (1,) * 3, kv_refs + own_refs):
        for n in range(count):
            k_cat[at : at + rows, :128] = ref[4 * n]
            k_cat[at : at + rows, 128:] = ref[4 * n + 1]
            v_cat[at : at + rows, :128] = ref[4 * n + 2]
            v_cat[at : at + rows, 128:] = ref[4 * n + 3]
            at += rows
    inverse = 128.0 ** -0.5
    chunk = 256
    total_rows = q_cat.shape[0]
    weight_sum = jnp.zeros((total_rows, 128), f32)
    dot_sum = jnp.zeros((total_rows, 128), f32)
    for at in range(0, k_cat.shape[0], chunk):
        keys = k_cat[at : at + chunk, :]
        scores = dot_nt(q_cat[:, 128:], keys[:, :128])
        scores_dot = dot_nt(q_cat[...], keys)
        weights = jnp.exp2(scores * (inverse * 1.4426950408889634))
        e_ref[:, at : at + chunk] = weights
        sd_ref[:, at : at + chunk] = scores_dot
        both = weights * scores_dot
        weight_sum += weights[:, :128] + weights[:, 128:]
        dot_sum += both[:, :128] + both[:, 128:]
    scale = 1.0 / jnp.sum(weight_sum, axis=-1, keepdims=True)
    center = jnp.sum(dot_sum, axis=-1, keepdims=True) * scale
    summed = jnp.zeros((total_rows, 256), f32)
    summed_dot = jnp.zeros((total_rows, 128), f32)
    for at in range(0, k_cat.shape[0], chunk):
        weights = e_ref[:, at : at + chunk]
        weights_dot = (weights * (sd_ref[:, at : at + chunk] - center)).astype(bf16)
        values = v_cat[at : at + chunk, :]
        summed += jnp.dot(weights.astype(bf16), values, preferred_element_type=f32)
        summed_dot += jnp.dot(weights_dot, values[:, :128], preferred_element_type=f32)
    primal = (summed[:, :128] * scale).astype(bf16)
    tangent = ((summed[:, 128:] + summed_dot * inverse) * scale).astype(bf16)
    for i in range(4):
        held_ref[i, :rows] = primal[i * rows : (i + 1) * rows]
        held_ref[i, rows:] = tangent[i * rows : (i + 1) * rows]
    for i, ref in enumerate(out_refs):
        ref[...] = held_ref[spot_ref[i]]


def attend(spot, key_parts, own_parts, first_queries):
    counts = tuple(part.shape[0] // 4 for part in key_parts)
    keys = 128 * (sum(counts) + 3)
    return pl.pallas_call(
        functools.partial(attend_kernel, counts),
        in_specs=[smem] + [vmem] * (len(counts) + 4),
        out_specs=[vmem] * 4,
        out_shape=[jax.ShapeDtypeStruct((256, 128), bf16)] * 4,
        scratch_shapes=[
            pltpu.VMEM((512, 256), bf16),
            pltpu.VMEM((keys, 256), bf16),
            pltpu.VMEM((keys, 256), bf16),
            pltpu.VMEM((512, keys), f32),
            pltpu.VMEM((512, keys), f32),
            pltpu.VMEM((4, 256, 128), bf16),
        ],
        compiler_params=pltpu.CompilerParams(vmem_limit_bytes=24 * MIB),
        cost_estimate=pl.CostEstimate(
            flops=2 * 512 * keys * 128 * 6, bytes_accessed=3 * MIB, transcendentals=512 * keys
        ),
    )(spot, *key_parts, *own_parts, first_queries)


def terms_kernel(spot_ref, h0, h1, h2, h3, own_ref, other_ref, *out_refs):
    y, zh, c = (spot_ref[i] for i in range(3))
    *out_refs, held_ref = out_refs
    for i, ref in enumerate((h0, h1, h2, h3)):
        held_ref[i] = ref[...]
    lefts = []
    for first, w_ref in ((2 * c, own_ref), (2 - 2 * c, other_ref)):
        left = jnp.concatenate([held_ref[(zh - first + 4) % 4], held_ref[(zh - first + 3) % 4]], axis=1)
        lefts.append((left, w_ref))
    for k, ref in enumerate(out_refs):
        total = None
        for left, w_ref in lefts:
            weight = w_ref[(y + k) % 4].reshape(-1, left.shape[1])
            term = dot_nt(left, weight)
            total = term if total is None else total + term
        ref[...] = total.astype(ref.dtype)


def terms(spot, heads, own, other):
    rows, cols = heads[0].shape[0], own.shape[1] * own.shape[2]
    kinds = [f32, bf16, bf16, bf16]
    return pl.pallas_call(
        terms_kernel,
        in_specs=[smem] + [vmem] * 6,
        out_specs=[vmem] * 4,
        out_shape=[jax.ShapeDtypeStruct((rows, cols), kind) for kind in kinds],
        scratch_shapes=[pltpu.VMEM((4,) + heads[0].shape, bf16)],
        compiler_params=pltpu.CompilerParams(vmem_limit_bytes=24 * MIB),
        cost_estimate=pl.CostEstimate(flops=2 * rows * 4 * cols * 512, bytes_accessed=6 * MIB, transcendentals=0),
    )(spot, *heads, own, other)


def finish_kernel(t0, t1, t2, t3, tok_ref, tan_ref, gate_ref, out_ref, out_dot_ref):
    rows = tok_ref.shape[0]
    total = t0[...] + t1[...].astype(f32) + t2[...].astype(f32) + t3[...].astype(f32)
    gate = gate_ref[...]
    out_ref[...] = (tok_ref[...].astype(f32) + gate * total[:rows]).astype(bf16)
    out_dot_ref[...] = (tan_ref[...].astype(f32) + gate * total[rows:]).astype(bf16)


def finish(parts, tokens, tangents, gate):
    rows, cols = tokens.shape
    return pl.pallas_call(
        finish_kernel,
        in_specs=[vmem] * 7,
        out_specs=[vmem] * 2,
        out_shape=[jax.ShapeDtypeStruct((rows, cols), bf16)] * 2,
        compiler_params=pltpu.CompilerParams(vmem_limit_bytes=24 * MIB),
        cost_estimate=pl.CostEstimate(flops=8 * rows * cols, bytes_accessed=3 * MIB, transcendentals=0),
    )(*parts, tokens, tangents, gate)


def from_ahead(array, axis, k):
    if k % 4 == 0:
        return array
    return lax.ppermute(array, axis, [(i, (i - k) % 4) for i in range(4)])


def swap(array, axis):
    return lax.ppermute(array, axis, [(0, 1), (1, 0)])


def beside(array, axis, sign):
    perm = [(2 * i + core, 2 * ((i - sign * (1 - 2 * core)) % 4) + core) for i in range(4) for core in range(2)]
    return lax.ppermute(array, (axis, "c"), perm)


def pick(array, index, axis=0):
    return lax.dynamic_index_in_dim(array, index, axis, keepdims=False)


def place(pieces, positions):
    out = jnp.zeros((len(pieces),) + pieces[0].shape, pieces[0].dtype)
    for piece, position in zip(pieces, positions):
        out = lax.dynamic_update_index_in_dim(out, piece, position, 0)
    return out


def after(array, *others):
    return lax.optimization_barrier((array,) + others)[0]


def per_device(tokens, tangents, qkv_weight, out_weight, mod_shift, mod_scale, mod_gate, query_gain, key_gain):
    zh, x, y = (lax.axis_index(name) for name in ("zh", "x", "y"))
    zl, c = lax.axis_index("zl"), lax.axis_index("c")
    clip = 2 * zl + c
    rows, features = tokens.shape
    share = features // 4
    ahead = lambda base, k: (base + k) % 4

    side = 1 - 2 * c
    ring = lambda base: [base, (base + side) % 4, (base + 2) % 4, (base - side) % 4]

    normed, quarter = modulate(y, tokens, tangents, mod_shift, mod_scale)
    normed = normed.reshape(4, 2 * rows, share)
    own_weight = pick(qkv_weight, clip, 1).reshape(qkv_weight.shape[0], 384)
    half = lax.dynamic_slice_in_dim(out_weight, 2 * c, 2, 1).reshape(-1, 256)
    near = swap(normed, "c")
    quarter = swap(quarter.reshape(2 * rows, share), "zl")
    near, quarter, own_weight = lax.optimization_barrier((near, quarter, own_weight))

    far_own = lax.all_gather(quarter, "y")
    columns = place([from_ahead(own_weight, "zh", k) for k in range(4)], [ahead(zh, k) for k in range(4)])
    columns = columns.reshape(-1, 384)
    up, down = beside(columns, "x", 1), beside(columns, "x", -1)
    up, down = lax.optimization_barrier((up, down))
    opposite = beside(up, "x", 1)
    far_other = swap(after(far_own, up, down), "c")

    spot = jnp.stack([x, (side + 4) % 4]).astype(jnp.int32)
    three = [columns, up, down]
    near_total = project_three(spot, [normed, near], three)
    far_total = project_three(spot, [far_own, far_other], three)
    gains = jnp.stack([query_gain, key_gain])
    spot = jnp.stack([ahead(x, 2)] + [ahead(zh, k) ^ clip for k in range(4)]).astype(jnp.int32)
    first, *blocks, first_queries = project_last(
        spot, [normed, near, far_own, far_other], opposite, near_total, far_total, gains
    )

    own = lax.all_gather(after(half, up, down), ("zh", "x"))

    def along_x(group):
        return [from_ahead(group, "x", m) for m in range(1, 4)]

    got = {k: from_ahead(blocks[k - 1], "zh", -k) for k in (1, 3)}
    second = along_x(first)
    wave = lax.optimization_barrier((got[1], got[3], *second))
    got[1], got[3], second = wave[0], wave[1], wave[2:]
    got[2] = from_ahead(after(blocks[1], *wave), "zh", -2)
    third = along_x(jnp.concatenate([got[1][:4], got[3][:4]]))
    got[2], third[0] = lax.optimization_barrier((got[2], third[0]))
    fourth = along_x(got[2][:4])
    spot = jnp.stack([ahead(zh, -clip - i) for i in range(4)]).astype(jnp.int32)
    own = own.reshape(4, 4, -1, 256)
    attended = attend(spot, [first, *second, *third, *fourth], [got[k] for k in (1, 2, 3)], first_queries)
    other = swap(after(own, attended[0]), "c")

    heads = []
    for i in range(4):
        perm = [(a * 4 + j, ((j + i) % 4) * 4 + a) for a in range(4) for j in range(4)]
        heads.append(lax.ppermute(attended[i], ("zh", "zl", "c"), perm))
    spot = jnp.stack([y, zh, c]).astype(jnp.int32)
    sums = terms(spot, heads, own, other)
    sums = [from_ahead(part, "y", -k) for k, part in enumerate(sums)]

    offset = y * share
    tokens_part = lax.dynamic_slice_in_dim(tokens, offset, share, 1)
    tangents_part = lax.dynamic_slice_in_dim(tangents, offset, share, 1)
    gate_part = lax.dynamic_slice_in_dim(mod_gate, offset, share, 0).reshape(1, share)
    result, result_tangent = finish(sums, tokens_part, tangents_part, gate_part)
    return (result, result_tangent)


def solution(mesh):
    split = Mesh(mesh.devices.reshape(4, 4, 4, 2, 2), ("zh", "x", "y", "zl", "c"))
    rows = P(("zl", "c", "zh", "x"), None)
    clip = P(("zl", "c"))
    return jax.shard_map(
        per_device,
        mesh=split,
        in_specs=(
            rows,
            rows,
            P(("zh", "x"), "y", None, None),
            P(("zh", "x"), "y", None),
            clip,
            clip,
            clip,
            P(),
            P(),
        ),
        out_specs=(P(("zl", "c", "zh", "x"), "y"), P(("zl", "c", "zh", "x"), "y")),
        check_vma=False,
    )
```

```python
import functools

import jax
import jax.numpy as jnp
from jax import lax
from jax.experimental import pallas as pl
from jax.experimental.pallas import tpu as pltpu
from jax.sharding import Mesh, PartitionSpec as P

epsilon = 1e-06
MIB = 1 << 20
f32 = jnp.float32
bf16 = jnp.bfloat16


def dot_nt(a, b):
    return lax.dot_general(a, b, (((1,), (1,)), ((), ())), preferred_element_type=f32)


def modulate_kernel(y_ref, tok_ref, tan_ref, shift_ref, scale_ref, out_ref, quarter_ref):
    groups, _, _, width = out_ref.shape
    part = width // groups
    gain = 1.0 + scale_ref[...]
    values = tok_ref[...].astype(f32)
    dots = tan_ref[...].astype(f32)
    center = values - jnp.mean(values, axis=-1, keepdims=True)
    center_dot = dots - jnp.mean(dots, axis=-1, keepdims=True)
    spread = jnp.mean(center * center, axis=-1, keepdims=True)
    spread_dot = 2.0 * jnp.mean(center * center_dot, axis=-1, keepdims=True)
    root = lax.rsqrt(spread + epsilon)
    root_dot = -0.5 * root * root * root * spread_dot
    normed = (center * root * gain + shift_ref[...]).astype(bf16)
    normed_dot = ((center_dot * root + center * root_dot) * gain).astype(bf16)
    for high in range(groups):
        for low in range(groups):
            start = (high * groups + low) * part
            out_ref[low, 0, :, high * part : (high + 1) * part] = normed[:, start : start + part]
            out_ref[low, 1, :, high * part : (high + 1) * part] = normed_dot[:, start : start + part]
    quarter_ref[...] = out_ref[y_ref[0]]


def modulate(y, tokens, tangents, shift, scale):
    rows, width = tokens.shape
    step = 32
    token_spec = pl.BlockSpec((step, width), lambda i, s: (i, 0))
    whole_spec = pl.BlockSpec((1, width), lambda i, s: (0, 0))
    return pl.pallas_call(
        modulate_kernel,
        grid_spec=pltpu.PrefetchScalarGridSpec(
            num_scalar_prefetch=1,
            grid=(rows // step,),
            in_specs=[token_spec, token_spec, whole_spec, whole_spec],
            out_specs=[
                pl.BlockSpec((4, 2, step, width // 4), lambda i, s: (0, 0, i, 0)),
                pl.BlockSpec((2, step, width // 4), lambda i, s: (0, i, 0)),
            ],
        ),
        out_shape=[
            jax.ShapeDtypeStruct((4, 2, rows, width // 4), bf16),
            jax.ShapeDtypeStruct((2, rows, width // 4), bf16),
        ],
        compiler_params=pltpu.CompilerParams(vmem_limit_bytes=56 * MIB),
        cost_estimate=pl.CostEstimate(flops=20 * rows * width, bytes_accessed=8 * rows * width, transcendentals=0),
    )(y.reshape(1).astype(jnp.int32), tokens, tangents, shift.reshape(1, width), scale.reshape(1, width))


smem = pl.BlockSpec(memory_space=pltpu.SMEM)
vmem = pl.BlockSpec(memory_space=pltpu.VMEM)


def three_kernel(spot_ref, n0_ref, n1_ref, w0_ref, w1_ref, w3_ref, out_ref):
    x, s = spot_ref[0], spot_ref[1]
    for r, ref in enumerate((n0_ref, n1_ref)):
        total = None
        for n, w_ref in enumerate((w0_ref, w1_ref, w3_ref)):
            term = jnp.dot(ref[(x + (0, s, 4 - s)[n]) % 4], w_ref[...], preferred_element_type=f32)
            total = term if total is None else total + term
        out_ref[r] = total


def project_three(spot, parts, weights):
    shape = (2, parts[0].shape[1], weights[0].shape[1])
    return pl.pallas_call(
        three_kernel,
        in_specs=[smem] + [vmem] * 5,
        out_specs=vmem,
        out_shape=jax.ShapeDtypeStruct(shape, f32),
        compiler_params=pltpu.CompilerParams(vmem_limit_bytes=24 * MIB),
        cost_estimate=pl.CostEstimate(flops=2 * 3 * 768 * 512 * 384, bytes_accessed=6 * MIB, transcendentals=0),
    )(spot, *parts, *weights)


def last_kernel(spot_ref, n0_ref, n1_ref, n2_ref, n3_ref, w_ref, near_ref, far_ref, gain_ref, *refs):
    *out_refs, own_ref, held_ref = refs
    rows = n0_ref.shape[1] // 2
    for r, ref in enumerate((n0_ref, n1_ref, n2_ref, n3_ref)):
        before = near_ref[r] if r < 2 else far_ref[r - 2]
        total = before + jnp.dot(ref[0], w_ref[...], preferred_element_type=f32)
        for kind in range(3):
            part = total[:rows, kind * 128 : (kind + 1) * 128]
            part_dot = total[rows:, kind * 128 : (kind + 1) * 128]
            if kind < 2:
                root = lax.rsqrt(jnp.mean(part * part, axis=-1, keepdims=True) + epsilon)
                root_dot = -root * root * root * jnp.mean(part * part_dot, axis=-1, keepdims=True)
                gain = gain_ref[kind : kind + 1, :]
                part, part_dot = part * root * gain, (part_dot * root + part * root_dot) * gain
            at = (4, 0, 2)[kind]
            held_ref[r, at] = part.astype(bf16)
            held_ref[r, at + 1] = part_dot.astype(bf16)
    for k, ref in enumerate(out_refs):
        ref[...] = held_ref[spot_ref[1 + k], : ref.shape[0]]
    own_ref[...] = held_ref[spot_ref[1], 4:]


def project_last(spot, parts, weight, near, far, gains):
    groups, rows, depth = parts[0].shape
    whole = lambda shape: pl.BlockSpec(shape, lambda n, s: (0,) * len(shape))
    part_spec = pl.BlockSpec((1, rows, depth), lambda n, s: (s[0], 0, 0))
    extra = [weight, near, far, gains]
    shapes = [(4, rows // 2, 128)] + [(6, rows // 2, 128)] * 3 + [(2, rows // 2, 128)]
    return pl.pallas_call(
        last_kernel,
        grid_spec=pltpu.PrefetchScalarGridSpec(
            num_scalar_prefetch=1,
            grid=(1,),
            in_specs=[part_spec] * 4 + [whole(a.shape) for a in extra],
            out_specs=[whole(shape) for shape in shapes],
            scratch_shapes=[pltpu.VMEM((4, 6, rows // 2, 128), bf16)],
        ),
        out_shape=[jax.ShapeDtypeStruct(shape, bf16) for shape in shapes],
        compiler_params=pltpu.CompilerParams(vmem_limit_bytes=24 * MIB),
        cost_estimate=pl.CostEstimate(flops=8 * rows * depth * 384, bytes_accessed=5 * MIB, transcendentals=0),
    )(spot, *parts, *extra)


def attend_kernel(counts, spot_ref, *refs):
    kv_refs = refs[: len(counts)]
    own_refs = refs[len(counts) : len(counts) + 3]
    first_ref, *out_refs, q_cat, k_cat, v_cat, e_ref, sd_ref, held_ref = refs[len(counts) + 3 :]
    rows = 128
    for i, ref in enumerate((first_ref,) + own_refs):
        at = 0 if i == 0 else 4
        q_cat[i * rows : (i + 1) * rows, :128] = ref[at + 1]
        q_cat[i * rows : (i + 1) * rows, 128:] = ref[at]
    at = 0
    for count, ref in zip(counts + (1,) * 3, kv_refs + own_refs):
        for n in range(count):
            k_cat[at : at + rows, :128] = ref[4 * n]
            k_cat[at : at + rows, 128:] = ref[4 * n + 1]
            v_cat[at : at + rows, :128] = ref[4 * n + 2]
            v_cat[at : at + rows, 128:] = ref[4 * n + 3]
            at += rows
    inverse = 128.0 ** -0.5
    chunk = 256
    total_rows = q_cat.shape[0]
    weight_sum = jnp.zeros((total_rows, 128), f32)
    dot_sum = jnp.zeros((total_rows, 128), f32)
    for at in range(0, k_cat.shape[0], chunk):
        keys = k_cat[at : at + chunk, :]
        scores = dot_nt(q_cat[:, 128:], keys[:, :128])
        scores_dot = dot_nt(q_cat[...], keys)
        weights = jnp.exp2(scores * (inverse * 1.4426950408889634))
        e_ref[:, at : at + chunk] = weights
        sd_ref[:, at : at + chunk] = scores_dot
        both = weights * scores_dot
        weight_sum += weights[:, :128] + weights[:, 128:]
        dot_sum += both[:, :128] + both[:, 128:]
    scale = 1.0 / jnp.sum(weight_sum, axis=-1, keepdims=True)
    center = jnp.sum(dot_sum, axis=-1, keepdims=True) * scale
    summed = jnp.zeros((total_rows, 256), f32)
    summed_dot = jnp.zeros((total_rows, 128), f32)
    for at in range(0, k_cat.shape[0], chunk):
        weights = e_ref[:, at : at + chunk]
        weights_dot = (weights * (sd_ref[:, at : at + chunk] - center)).astype(bf16)
        values = v_cat[at : at + chunk, :]
        summed += jnp.dot(weights.astype(bf16), values, preferred_element_type=f32)
        summed_dot += jnp.dot(weights_dot, values[:, :128], preferred_element_type=f32)
    primal = (summed[:, :128] * scale).astype(bf16)
    tangent = ((summed[:, 128:] + summed_dot * inverse) * scale).astype(bf16)
    for i in range(4):
        held_ref[i, :rows] = primal[i * rows : (i + 1) * rows]
        held_ref[i, rows:] = tangent[i * rows : (i + 1) * rows]
    for i, ref in enumerate(out_refs):
        ref[...] = held_ref[spot_ref[i]]


def attend(spot, key_parts, own_parts, first_queries):
    counts = tuple(part.shape[0] // 4 for part in key_parts)
    keys = 128 * (sum(counts) + 3)
    return pl.pallas_call(
        functools.partial(attend_kernel, counts),
        in_specs=[smem] + [vmem] * (len(counts) + 4),
        out_specs=[vmem] * 4,
        out_shape=[jax.ShapeDtypeStruct((256, 128), bf16)] * 4,
        scratch_shapes=[
            pltpu.VMEM((512, 256), bf16),
            pltpu.VMEM((keys, 256), bf16),
            pltpu.VMEM((keys, 256), bf16),
            pltpu.VMEM((512, keys), f32),
            pltpu.VMEM((512, keys), f32),
            pltpu.VMEM((4, 256, 128), bf16),
        ],
        compiler_params=pltpu.CompilerParams(vmem_limit_bytes=24 * MIB),
        cost_estimate=pl.CostEstimate(
            flops=2 * 512 * keys * 128 * 6, bytes_accessed=3 * MIB, transcendentals=512 * keys
        ),
    )(spot, *key_parts, *own_parts, first_queries)


def finish_kernel(place_ref, h0, h1, h2, h3, own_ref, other_ref, tok_ref, tan_ref, gate_ref, out_ref, out_dot_ref):
    rows = tok_ref.shape[0]
    y, zh, c = (place_ref[i] for i in range(3))
    totals = [None] * own_ref.shape[1]
    for m, ref in enumerate((h0, h1, h2, h3)):
        for first, w_ref in ((2 * c, own_ref), (2 - 2 * c, other_ref)):
            left = jnp.concatenate([ref[(zh - first + 4) % 4], ref[(zh - first + 3) % 4]], axis=1)
            for b in range(len(totals)):
                term = dot_nt(left, w_ref[(y + m) % 4, b])
                totals[b] = term if totals[b] is None else totals[b] + term
    total = jnp.concatenate(totals, axis=1)
    gate = gate_ref[...]
    out_ref[...] = (tok_ref[...].astype(f32) + gate * total[:rows]).astype(bf16)
    out_dot_ref[...] = (tan_ref[...].astype(f32) + gate * total[rows:]).astype(bf16)


def finish(place, parts, own, other, tokens, tangents, gate):
    rows, cols = tokens.shape
    step = cols // 2
    part_spec = pl.BlockSpec(parts[0].shape, lambda n, s: (0, 0, 0))
    col_spec = pl.BlockSpec((rows, step), lambda n, s: (0, n))
    weight_spec = pl.BlockSpec((4, 2) + own.shape[2:], lambda n, s: (0, n, 0, 0))
    return pl.pallas_call(
        finish_kernel,
        grid_spec=pltpu.PrefetchScalarGridSpec(
            num_scalar_prefetch=1,
            grid=(2,),
            in_specs=[part_spec] * 4
            + [weight_spec, weight_spec, col_spec, col_spec, pl.BlockSpec((1, step), lambda n, s: (0, n))],
            out_specs=[col_spec, col_spec],
        ),
        out_shape=[jax.ShapeDtypeStruct((rows, cols), bf16)] * 2,
        compiler_params=pltpu.CompilerParams(vmem_limit_bytes=56 * MIB),
        cost_estimate=pl.CostEstimate(flops=4 * rows * cols * 2048, bytes_accessed=6 * MIB, transcendentals=0),
    )(place, *parts, own, other, tokens, tangents, gate)


def from_ahead(array, axis, k):
    if k % 4 == 0:
        return array
    return lax.ppermute(array, axis, [(i, (i - k) % 4) for i in range(4)])


def swap(array, axis):
    return lax.ppermute(array, axis, [(0, 1), (1, 0)])


def beside(array, axis, sign):
    perm = [(2 * i + core, 2 * ((i - sign * (1 - 2 * core)) % 4) + core) for i in range(4) for core in range(2)]
    return lax.ppermute(array, (axis, "c"), perm)


def pick(array, index, axis=0):
    return lax.dynamic_index_in_dim(array, index, axis, keepdims=False)


def place(pieces, positions):
    out = jnp.zeros((len(pieces),) + pieces[0].shape, pieces[0].dtype)
    for piece, position in zip(pieces, positions):
        out = lax.dynamic_update_index_in_dim(out, piece, position, 0)
    return out


def after(array, *others):
    return lax.optimization_barrier((array,) + others)[0]


def per_device(tokens, tangents, qkv_weight, out_weight, mod_shift, mod_scale, mod_gate, query_gain, key_gain):
    zh, x, y = (lax.axis_index(name) for name in ("zh", "x", "y"))
    zl, c = lax.axis_index("zl"), lax.axis_index("c")
    clip = 2 * zl + c
    rows, features = tokens.shape
    share = features // 4
    ahead = lambda base, k: (base + k) % 4

    side = 1 - 2 * c
    ring = lambda base: [base, (base + side) % 4, (base + 2) % 4, (base - side) % 4]

    normed, quarter = modulate(y, tokens, tangents, mod_shift, mod_scale)
    normed = normed.reshape(4, 2 * rows, share)
    own_weight = pick(qkv_weight, clip, 1).reshape(qkv_weight.shape[0], 384)
    half = lax.dynamic_slice_in_dim(out_weight, 2 * c, 2, 1).reshape(-1, 256)
    near = swap(normed, "c")
    quarter = swap(quarter.reshape(2 * rows, share), "zl")
    near, quarter, own_weight = lax.optimization_barrier((near, quarter, own_weight))

    far_own = lax.all_gather(quarter, "y")
    columns = place([from_ahead(own_weight, "zh", k) for k in range(4)], [ahead(zh, k) for k in range(4)])
    columns = columns.reshape(-1, 384)
    up, down = beside(columns, "x", 1), beside(columns, "x", -1)
    half = after(half, columns)
    half = lax.ppermute(half, ("zh", "y"), [(a * 4 + b, b * 4 + a) for a in range(4) for b in range(4)])
    up, down, half = lax.optimization_barrier((up, down, half))
    opposite = beside(up, "x", 1)
    far_other = swap(after(far_own, up, down), "c")

    spot = jnp.stack([x, (side + 4) % 4]).astype(jnp.int32)
    three = [columns, up, down]
    near_total = project_three(spot, [normed, near], three)
    far_total = project_three(spot, [far_own, far_other], three)
    gains = jnp.stack([query_gain, key_gain])
    spot = jnp.stack([ahead(x, 2)] + [ahead(zh, k) ^ clip for k in range(4)]).astype(jnp.int32)
    first, *blocks, first_queries = project_last(
        spot, [normed, near, far_own, far_other], opposite, near_total, far_total, gains
    )

    half_rows = lax.all_gather(half, ("zh", "x"))

    def along_x(group):
        return [from_ahead(group, "x", m) for m in range(1, 4)]

    got = {k: from_ahead(blocks[k - 1], "zh", -k) for k in (1, 3)}
    second = along_x(first)
    wave = lax.optimization_barrier((got[1], got[3], *second))
    got[1], got[3], second = wave[0], wave[1], wave[2:]
    got[2] = from_ahead(after(blocks[1], *wave), "zh", -2)
    third = along_x(jnp.concatenate([got[1][:4], got[3][:4]]))
    got[2], third[0] = lax.optimization_barrier((got[2], third[0]))
    fourth = along_x(got[2][:4])
    spot = jnp.stack([ahead(zh, -clip - i) for i in range(4)]).astype(jnp.int32)
    attended = attend(spot, [first, *second, *third, *fourth], [got[k] for k in (1, 2, 3)], first_queries)

    heads = []
    for i in range(4):
        perm = [(a * 4 + j, ((j + i) % 4) * 4 + a) for a in range(4) for j in range(4)]
        heads.append(lax.ppermute(attended[i], ("zh", "zl", "c"), perm))
    heads = jnp.stack(heads)
    all_heads = [from_ahead(heads, "y", m) for m in range(4)]
    own = half_rows.reshape(4, 4, -1, 256)
    other = swap(after(own, heads), "c")

    offset = y * share
    tokens_part = lax.dynamic_slice_in_dim(tokens, offset, share, 1)
    tangents_part = lax.dynamic_slice_in_dim(tangents, offset, share, 1)
    gate_part = lax.dynamic_slice_in_dim(mod_gate, offset, share, 0).reshape(1, share)
    spot = jnp.stack([y, zh, c]).astype(jnp.int32)
    result, result_tangent = finish(spot, all_heads, own, other, tokens_part, tangents_part, gate_part)
    return (result, result_tangent)


def solution(mesh):
    split = Mesh(mesh.devices.reshape(4, 4, 4, 2, 2), ("zh", "x", "y", "zl", "c"))
    rows = P(("zl", "c", "zh", "x"), None)
    clip = P(("zl", "c"))
    return jax.shard_map(
        per_device,
        mesh=split,
        in_specs=(
            rows,
            rows,
            P(("zh", "x"), "y", None, None),
            P(("zh", "x"), "y", None),
            clip,
            clip,
            clip,
            P(),
            P(),
        ),
        out_specs=(P(("zl", "c", "zh", "x"), "y"), P(("zl", "c", "zh", "x"), "y")),
        check_vma=False,
    )
```

```python
import functools

import jax
import jax.numpy as jnp
from jax import lax
from jax.experimental import pallas as pl
from jax.experimental.pallas import tpu as pltpu
from jax.sharding import Mesh, PartitionSpec as P

epsilon = 1e-06
MIB = 1 << 20
f32 = jnp.float32
bf16 = jnp.bfloat16


def dot_nt(a, b):
    return lax.dot_general(a, b, (((1,), (1,)), ((), ())), preferred_element_type=f32)


def modulate_kernel(y_ref, tok_ref, tan_ref, shift_ref, scale_ref, out_ref, quarter_ref):
    groups, _, _, width = out_ref.shape
    part = width // groups
    gain = 1.0 + scale_ref[...]
    values = tok_ref[...].astype(f32)
    dots = tan_ref[...].astype(f32)
    center = values - jnp.mean(values, axis=-1, keepdims=True)
    center_dot = dots - jnp.mean(dots, axis=-1, keepdims=True)
    spread = jnp.mean(center * center, axis=-1, keepdims=True)
    spread_dot = 2.0 * jnp.mean(center * center_dot, axis=-1, keepdims=True)
    root = lax.rsqrt(spread + epsilon)
    root_dot = -0.5 * root * root * root * spread_dot
    normed = (center * root * gain + shift_ref[...]).astype(bf16)
    normed_dot = ((center_dot * root + center * root_dot) * gain).astype(bf16)
    for high in range(groups):
        for low in range(groups):
            start = (high * groups + low) * part
            out_ref[low, 0, :, high * part : (high + 1) * part] = normed[:, start : start + part]
            out_ref[low, 1, :, high * part : (high + 1) * part] = normed_dot[:, start : start + part]
    quarter_ref[...] = out_ref[y_ref[0]]


def modulate(y, tokens, tangents, shift, scale):
    rows, width = tokens.shape
    step = 64
    token_spec = pl.BlockSpec((step, width), lambda i, s: (i, 0))
    whole_spec = pl.BlockSpec((1, width), lambda i, s: (0, 0))
    return pl.pallas_call(
        modulate_kernel,
        grid_spec=pltpu.PrefetchScalarGridSpec(
            num_scalar_prefetch=1,
            grid=(rows // step,),
            in_specs=[token_spec, token_spec, whole_spec, whole_spec],
            out_specs=[
                pl.BlockSpec((4, 2, step, width // 4), lambda i, s: (0, 0, i, 0)),
                pl.BlockSpec((2, step, width // 4), lambda i, s: (0, i, 0)),
            ],
        ),
        out_shape=[
            jax.ShapeDtypeStruct((4, 2, rows, width // 4), bf16),
            jax.ShapeDtypeStruct((2, rows, width // 4), bf16),
        ],
        compiler_params=pltpu.CompilerParams(vmem_limit_bytes=56 * MIB),
        cost_estimate=pl.CostEstimate(flops=20 * rows * width, bytes_accessed=8 * rows * width, transcendentals=0),
    )(y.reshape(1).astype(jnp.int32), tokens, tangents, shift.reshape(1, width), scale.reshape(1, width))


smem = pl.BlockSpec(memory_space=pltpu.SMEM)
vmem = pl.BlockSpec(memory_space=pltpu.VMEM)


def three_kernel(spot_ref, n0_ref, n1_ref, w0_ref, w1_ref, w3_ref, out_ref):
    x, s = spot_ref[0], spot_ref[1]
    for r, ref in enumerate((n0_ref, n1_ref)):
        total = None
        for n, w_ref in enumerate((w0_ref, w1_ref, w3_ref)):
            term = jnp.dot(ref[(x + (0, s, 4 - s)[n]) % 4], w_ref[...], preferred_element_type=f32)
            total = term if total is None else total + term
        out_ref[r] = total


def project_three(spot, parts, weights):
    shape = (2, parts[0].shape[1], weights[0].shape[1])
    return pl.pallas_call(
        three_kernel,
        in_specs=[smem] + [vmem] * 5,
        out_specs=vmem,
        out_shape=jax.ShapeDtypeStruct(shape, f32),
        compiler_params=pltpu.CompilerParams(vmem_limit_bytes=24 * MIB),
        cost_estimate=pl.CostEstimate(flops=2 * 3 * 768 * 512 * 384, bytes_accessed=6 * MIB, transcendentals=0),
    )(spot, *parts, *weights)


def last_kernel(spot_ref, n0_ref, n1_ref, n2_ref, n3_ref, w_ref, near_ref, far_ref, gain_ref, *refs):
    *out_refs, own_ref, held_ref = refs
    rows = n0_ref.shape[1] // 2
    for r, ref in enumerate((n0_ref, n1_ref, n2_ref, n3_ref)):
        before = near_ref[r] if r < 2 else far_ref[r - 2]
        total = before + jnp.dot(ref[0], w_ref[...], preferred_element_type=f32)
        for kind in range(3):
            part = total[:rows, kind * 128 : (kind + 1) * 128]
            part_dot = total[rows:, kind * 128 : (kind + 1) * 128]
            if kind < 2:
                root = lax.rsqrt(jnp.mean(part * part, axis=-1, keepdims=True) + epsilon)
                root_dot = -root * root * root * jnp.mean(part * part_dot, axis=-1, keepdims=True)
                gain = gain_ref[kind : kind + 1, :]
                part, part_dot = part * root * gain, (part_dot * root + part * root_dot) * gain
            at = (4, 0, 2)[kind]
            held_ref[r, at] = part.astype(bf16)
            held_ref[r, at + 1] = part_dot.astype(bf16)
    for k, ref in enumerate(out_refs):
        ref[...] = held_ref[spot_ref[1 + k], : ref.shape[0]]
    own_ref[...] = held_ref[spot_ref[1], 4:]


def project_last(spot, parts, weight, near, far, gains):
    groups, rows, depth = parts[0].shape
    whole = lambda shape: pl.BlockSpec(shape, lambda n, s: (0,) * len(shape))
    part_spec = pl.BlockSpec((1, rows, depth), lambda n, s: (s[0], 0, 0))
    extra = [weight, near, far, gains]
    shapes = [(4, rows // 2, 128)] + [(6, rows // 2, 128)] * 3 + [(2, rows // 2, 128)]
    return pl.pallas_call(
        last_kernel,
        grid_spec=pltpu.PrefetchScalarGridSpec(
            num_scalar_prefetch=1,
            grid=(1,),
            in_specs=[part_spec] * 4 + [whole(a.shape) for a in extra],
            out_specs=[whole(shape) for shape in shapes],
            scratch_shapes=[pltpu.VMEM((4, 6, rows // 2, 128), bf16)],
        ),
        out_shape=[jax.ShapeDtypeStruct(shape, bf16) for shape in shapes],
        compiler_params=pltpu.CompilerParams(vmem_limit_bytes=24 * MIB),
        cost_estimate=pl.CostEstimate(flops=8 * rows * depth * 384, bytes_accessed=5 * MIB, transcendentals=0),
    )(spot, *parts, *extra)


def attend_kernel(counts, spot_ref, *refs):
    kv_refs = refs[: len(counts)]
    own_refs = refs[len(counts) : len(counts) + 3]
    first_ref, *out_refs, q_cat, k_cat, v_cat, e_ref, sd_ref, held_ref = refs[len(counts) + 3 :]
    rows = 128
    for i, ref in enumerate((first_ref,) + own_refs):
        at = 0 if i == 0 else 4
        q_cat[i * rows : (i + 1) * rows, :128] = ref[at + 1]
        q_cat[i * rows : (i + 1) * rows, 128:] = ref[at]
    at = 0
    for count, ref in zip(counts + (1,) * 3, kv_refs + own_refs):
        for n in range(count):
            k_cat[at : at + rows, :128] = ref[4 * n]
            k_cat[at : at + rows, 128:] = ref[4 * n + 1]
            v_cat[at : at + rows, :128] = ref[4 * n + 2]
            v_cat[at : at + rows, 128:] = ref[4 * n + 3]
            at += rows
    inverse = 128.0 ** -0.5
    chunk = 256
    total_rows = q_cat.shape[0]
    weight_sum = jnp.zeros((total_rows, 128), f32)
    dot_sum = jnp.zeros((total_rows, 128), f32)
    for at in range(0, k_cat.shape[0], chunk):
        keys = k_cat[at : at + chunk, :]
        scores = dot_nt(q_cat[:, 128:], keys[:, :128])
        scores_dot = dot_nt(q_cat[...], keys)
        weights = jnp.exp2(scores * (inverse * 1.4426950408889634))
        e_ref[:, at : at + chunk] = weights
        sd_ref[:, at : at + chunk] = scores_dot
        both = weights * scores_dot
        weight_sum += weights[:, :128] + weights[:, 128:]
        dot_sum += both[:, :128] + both[:, 128:]
    scale = 1.0 / jnp.sum(weight_sum, axis=-1, keepdims=True)
    center = jnp.sum(dot_sum, axis=-1, keepdims=True) * scale
    summed = jnp.zeros((total_rows, 256), f32)
    summed_dot = jnp.zeros((total_rows, 128), f32)
    for at in range(0, k_cat.shape[0], chunk):
        weights = e_ref[:, at : at + chunk]
        weights_dot = (weights * (sd_ref[:, at : at + chunk] - center)).astype(bf16)
        values = v_cat[at : at + chunk, :]
        summed += jnp.dot(weights.astype(bf16), values, preferred_element_type=f32)
        summed_dot += jnp.dot(weights_dot, values[:, :128], preferred_element_type=f32)
    primal = (summed[:, :128] * scale).astype(bf16)
    tangent = ((summed[:, 128:] + summed_dot * inverse) * scale).astype(bf16)
    for i in range(4):
        held_ref[i, :rows] = primal[i * rows : (i + 1) * rows]
        held_ref[i, rows:] = tangent[i * rows : (i + 1) * rows]
    for i, ref in enumerate(out_refs):
        ref[...] = held_ref[spot_ref[i]]


def attend(spot, key_parts, own_parts, first_queries):
    counts = tuple(part.shape[0] // 4 for part in key_parts)
    keys = 128 * (sum(counts) + 3)
    return pl.pallas_call(
        functools.partial(attend_kernel, counts),
        in_specs=[smem] + [vmem] * (len(counts) + 4),
        out_specs=[vmem] * 4,
        out_shape=[jax.ShapeDtypeStruct((256, 128), bf16)] * 4,
        scratch_shapes=[
            pltpu.VMEM((512, 256), bf16),
            pltpu.VMEM((keys, 256), bf16),
            pltpu.VMEM((keys, 256), bf16),
            pltpu.VMEM((512, keys), f32),
            pltpu.VMEM((512, keys), f32),
            pltpu.VMEM((4, 256, 128), bf16),
        ],
        compiler_params=pltpu.CompilerParams(vmem_limit_bytes=24 * MIB),
        cost_estimate=pl.CostEstimate(
            flops=2 * 512 * keys * 128 * 6, bytes_accessed=3 * MIB, transcendentals=512 * keys
        ),
    )(spot, *key_parts, *own_parts, first_queries)


def finish_kernel(place_ref, h0, h1, h2, h3, own_ref, other_ref, tok_ref, tan_ref, gate_ref, out_ref, out_dot_ref):
    rows = tok_ref.shape[0]
    y, zh, c = (place_ref[i] for i in range(3))
    total = None
    for m, ref in enumerate((h0, h1, h2, h3)):
        for first, w_ref in ((2 * c, own_ref), (2 - 2 * c, other_ref)):
            left = jnp.concatenate([ref[(zh - first + 4) % 4], ref[(zh - first + 3) % 4]], axis=1)
            term = dot_nt(left, w_ref[(y + m) % 4].reshape(-1, left.shape[1]))
            total = term if total is None else total + term
    gate = gate_ref[...]
    out_ref[...] = (tok_ref[...].astype(f32) + gate * total[:rows]).astype(bf16)
    out_dot_ref[...] = (tan_ref[...].astype(f32) + gate * total[rows:]).astype(bf16)


def finish(place, parts, own, other, tokens, tangents, gate):
    rows, cols = tokens.shape
    return pl.pallas_call(
        finish_kernel,
        in_specs=[smem] + [vmem] * 9,
        out_specs=[vmem] * 2,
        out_shape=[jax.ShapeDtypeStruct((rows, cols), bf16)] * 2,
        compiler_params=pltpu.CompilerParams(vmem_limit_bytes=24 * MIB),
        cost_estimate=pl.CostEstimate(flops=4 * rows * cols * 2048, bytes_accessed=6 * MIB, transcendentals=0),
    )(place, *parts, own, other, tokens, tangents, gate)


def from_ahead(array, axis, k):
    if k % 4 == 0:
        return array
    return lax.ppermute(array, axis, [(i, (i - k) % 4) for i in range(4)])


def swap(array, axis):
    return lax.ppermute(array, axis, [(0, 1), (1, 0)])


def beside(array, axis, sign):
    perm = [(2 * i + core, 2 * ((i - sign * (1 - 2 * core)) % 4) + core) for i in range(4) for core in range(2)]
    return lax.ppermute(array, (axis, "c"), perm)


def pick(array, index, axis=0):
    return lax.dynamic_index_in_dim(array, index, axis, keepdims=False)


def place(pieces, positions):
    out = jnp.zeros((len(pieces),) + pieces[0].shape, pieces[0].dtype)
    for piece, position in zip(pieces, positions):
        out = lax.dynamic_update_index_in_dim(out, piece, position, 0)
    return out


def after(array, *others):
    return lax.optimization_barrier((array,) + others)[0]


def per_device(tokens, tangents, qkv_weight, out_weight, mod_shift, mod_scale, mod_gate, query_gain, key_gain):
    zh, x, y = (lax.axis_index(name) for name in ("zh", "x", "y"))
    zl, c = lax.axis_index("zl"), lax.axis_index("c")
    clip = 2 * zl + c
    rows, features = tokens.shape
    share = features // 4
    ahead = lambda base, k: (base + k) % 4

    side = 1 - 2 * c
    ring = lambda base: [base, (base + side) % 4, (base + 2) % 4, (base - side) % 4]

    normed, quarter = modulate(y, tokens, tangents, mod_shift, mod_scale)
    normed = normed.reshape(4, 2 * rows, share)
    own_weight = pick(qkv_weight, clip, 1).reshape(qkv_weight.shape[0], 384)
    half = lax.dynamic_slice_in_dim(out_weight, 2 * c, 2, 1).reshape(-1, 256)
    near = swap(normed, "c")
    quarter = swap(quarter.reshape(2 * rows, share), "zl")
    near, quarter, own_weight = lax.optimization_barrier((near, quarter, own_weight))

    far_own = lax.all_gather(quarter, "y")
    columns = place([from_ahead(own_weight, "zh", k) for k in range(4)], [ahead(zh, k) for k in range(4)])
    columns = columns.reshape(-1, 384)
    up, down = beside(columns, "x", 1), beside(columns, "x", -1)
    half = after(half, columns)
    half = lax.ppermute(half, ("zh", "y"), [(a * 4 + b, b * 4 + a) for a in range(4) for b in range(4)])
    up, down, half = lax.optimization_barrier((up, down, half))
    opposite = beside(up, "x", 1)
    far_other = swap(after(far_own, up, down), "c")

    spot = jnp.stack([x, (side + 4) % 4]).astype(jnp.int32)
    three = [columns, up, down]
    near_total = project_three(spot, [normed, near], three)
    far_total = project_three(spot, [far_own, far_other], three)
    gains = jnp.stack([query_gain, key_gain])
    spot = jnp.stack([ahead(x, 2)] + [ahead(zh, k) ^ clip for k in range(4)]).astype(jnp.int32)
    first, *blocks, first_queries = project_last(
        spot, [normed, near, far_own, far_other], opposite, near_total, far_total, gains
    )

    half_rows = lax.all_gather(half, ("zh", "x"))

    def along_x(group):
        return [from_ahead(group, "x", m) for m in range(1, 4)]

    got = {k: from_ahead(blocks[k - 1], "zh", -k) for k in (1, 3)}
    second = along_x(first)
    got[1], middle_block, *second = lax.optimization_barrier((got[1], blocks[1], *second))
    wave = lax.optimization_barrier((got[1], got[3], *second))
    got[1], got[3], second = wave[0], wave[1], wave[2:]
    got[2] = from_ahead(middle_block, "zh", -2)
    third = along_x(jnp.concatenate([got[1][:4], got[3][:4]]))
    got[2], third[0] = lax.optimization_barrier((got[2], third[0]))
    fourth = along_x(got[2][:4])
    spot = jnp.stack([ahead(zh, -clip - i) for i in range(4)]).astype(jnp.int32)
    attended = attend(spot, [first, *second, *third, *fourth], [got[k] for k in (1, 2, 3)], first_queries)

    heads = []
    for i in range(4):
        perm = [(a * 4 + j, ((j + i) % 4) * 4 + a) for a in range(4) for j in range(4)]
        heads.append(lax.ppermute(attended[i], ("zh", "zl", "c"), perm))
    heads = jnp.stack(heads)
    all_heads = [from_ahead(heads, "y", m) for m in range(4)]
    own = half_rows.reshape(4, 4, -1, 256)
    other = swap(after(own, heads), "c")

    offset = y * share
    tokens_part = lax.dynamic_slice_in_dim(tokens, offset, share, 1)
    tangents_part = lax.dynamic_slice_in_dim(tangents, offset, share, 1)
    gate_part = lax.dynamic_slice_in_dim(mod_gate, offset, share, 0).reshape(1, share)
    spot = jnp.stack([y, zh, c]).astype(jnp.int32)
    result, result_tangent = finish(spot, all_heads, own, other, tokens_part, tangents_part, gate_part)
    return (result, result_tangent)


def solution(mesh):
    split = Mesh(mesh.devices.reshape(4, 4, 4, 2, 2), ("zh", "x", "y", "zl", "c"))
    rows = P(("zl", "c", "zh", "x"), None)
    clip = P(("zl", "c"))
    return jax.shard_map(
        per_device,
        mesh=split,
        in_specs=(
            rows,
            rows,
            P(("zh", "x"), "y", None, None),
            P(("zh", "x"), "y", None),
            clip,
            clip,
            clip,
            P(),
            P(),
        ),
        out_specs=(P(("zl", "c", "zh", "x"), "y"), P(("zl", "c", "zh", "x"), "y")),
        check_vma=False,
    )
```

```python
import functools

import jax
import jax.numpy as jnp
from jax import lax
from jax.experimental import pallas as pl
from jax.experimental.pallas import tpu as pltpu
from jax.sharding import Mesh, PartitionSpec as P

epsilon = 1e-06
MIB = 1 << 20
f32 = jnp.float32
bf16 = jnp.bfloat16


def dot_nt(a, b):
    return lax.dot_general(a, b, (((1,), (1,)), ((), ())), preferred_element_type=f32)


def modulate_kernel(y_ref, tok_ref, tan_ref, shift_ref, scale_ref, out_ref, quarter_ref):
    groups, _, _, width = out_ref.shape
    part = width // groups
    gain = 1.0 + scale_ref[...]
    values = tok_ref[...].astype(f32)
    dots = tan_ref[...].astype(f32)
    center = values - jnp.mean(values, axis=-1, keepdims=True)
    center_dot = dots - jnp.mean(dots, axis=-1, keepdims=True)
    spread = jnp.mean(center * center, axis=-1, keepdims=True)
    spread_dot = 2.0 * jnp.mean(center * center_dot, axis=-1, keepdims=True)
    root = lax.rsqrt(spread + epsilon)
    root_dot = -0.5 * root * root * root * spread_dot
    normed = (center * root * gain + shift_ref[...]).astype(bf16)
    normed_dot = ((center_dot * root + center * root_dot) * gain).astype(bf16)
    for high in range(groups):
        for low in range(groups):
            start = (high * groups + low) * part
            out_ref[low, 0, :, high * part : (high + 1) * part] = normed[:, start : start + part]
            out_ref[low, 1, :, high * part : (high + 1) * part] = normed_dot[:, start : start + part]
    quarter_ref[...] = out_ref[y_ref[0]]


def modulate(y, tokens, tangents, shift, scale):
    rows, width = tokens.shape
    step = 64
    token_spec = pl.BlockSpec((step, width), lambda i, s: (i, 0))
    whole_spec = pl.BlockSpec((1, width), lambda i, s: (0, 0))
    return pl.pallas_call(
        modulate_kernel,
        grid_spec=pltpu.PrefetchScalarGridSpec(
            num_scalar_prefetch=1,
            grid=(rows // step,),
            in_specs=[token_spec, token_spec, whole_spec, whole_spec],
            out_specs=[
                pl.BlockSpec((4, 2, step, width // 4), lambda i, s: (0, 0, i, 0)),
                pl.BlockSpec((2, step, width // 4), lambda i, s: (0, i, 0)),
            ],
        ),
        out_shape=[
            jax.ShapeDtypeStruct((4, 2, rows, width // 4), bf16),
            jax.ShapeDtypeStruct((2, rows, width // 4), bf16),
        ],
        compiler_params=pltpu.CompilerParams(vmem_limit_bytes=56 * MIB),
        cost_estimate=pl.CostEstimate(flops=20 * rows * width, bytes_accessed=8 * rows * width, transcendentals=0),
    )(y.reshape(1).astype(jnp.int32), tokens, tangents, shift.reshape(1, width), scale.reshape(1, width))


smem = pl.BlockSpec(memory_space=pltpu.SMEM)
vmem = pl.BlockSpec(memory_space=pltpu.VMEM)


def three_kernel(spot_ref, n0_ref, n1_ref, w0_ref, w1_ref, w3_ref, out_ref):
    x, s = spot_ref[0], spot_ref[1]
    for r, ref in enumerate((n0_ref, n1_ref)):
        total = None
        for n, w_ref in enumerate((w0_ref, w1_ref, w3_ref)):
            term = jnp.dot(ref[(x + (0, s, 4 - s)[n]) % 4], w_ref[...], preferred_element_type=f32)
            total = term if total is None else total + term
        out_ref[r] = total


def project_three(spot, parts, weights):
    shape = (2, parts[0].shape[1], weights[0].shape[1])
    return pl.pallas_call(
        three_kernel,
        in_specs=[smem] + [vmem] * 5,
        out_specs=vmem,
        out_shape=jax.ShapeDtypeStruct(shape, f32),
        compiler_params=pltpu.CompilerParams(vmem_limit_bytes=24 * MIB),
        cost_estimate=pl.CostEstimate(flops=2 * 3 * 768 * 512 * 384, bytes_accessed=6 * MIB, transcendentals=0),
    )(spot, *parts, *weights)


def last_kernel(spot_ref, n0_ref, n1_ref, n2_ref, n3_ref, w_ref, near_ref, far_ref, gain_ref, *refs):
    *out_refs, held_ref = refs
    rows = n0_ref.shape[1] // 2
    for r, ref in enumerate((n0_ref, n1_ref, n2_ref, n3_ref)):
        before = near_ref[r] if r < 2 else far_ref[r - 2]
        total = before + jnp.dot(ref[0], w_ref[...], preferred_element_type=f32)
        for kind in range(3):
            part = total[:rows, kind * 128 : (kind + 1) * 128]
            part_dot = total[rows:, kind * 128 : (kind + 1) * 128]
            if kind < 2:
                root = lax.rsqrt(jnp.mean(part * part, axis=-1, keepdims=True) + epsilon)
                root_dot = -root * root * root * jnp.mean(part * part_dot, axis=-1, keepdims=True)
                gain = gain_ref[kind : kind + 1, :]
                part, part_dot = part * root * gain, (part_dot * root + part * root_dot) * gain
            at = (4, 0, 2)[kind]
            held_ref[r, at] = part.astype(bf16)
            held_ref[r, at + 1] = part_dot.astype(bf16)
    for k in range(4):
        out_refs[k][...] = held_ref[spot_ref[1 + k], :4]
        out_refs[4 + k][...] = held_ref[spot_ref[1 + k], 4:]


def project_last(spot, parts, weight, near, far, gains):
    groups, rows, depth = parts[0].shape
    whole = lambda shape: pl.BlockSpec(shape, lambda n, s: (0,) * len(shape))
    part_spec = pl.BlockSpec((1, rows, depth), lambda n, s: (s[0], 0, 0))
    extra = [weight, near, far, gains]
    shapes = [(4, rows // 2, 128)] * 4 + [(2, rows // 2, 128)] * 4
    return pl.pallas_call(
        last_kernel,
        grid_spec=pltpu.PrefetchScalarGridSpec(
            num_scalar_prefetch=1,
            grid=(1,),
            in_specs=[part_spec] * 4 + [whole(a.shape) for a in extra],
            out_specs=[whole(shape) for shape in shapes],
            scratch_shapes=[pltpu.VMEM((4, 6, rows // 2, 128), bf16)],
        ),
        out_shape=[jax.ShapeDtypeStruct(shape, bf16) for shape in shapes],
        compiler_params=pltpu.CompilerParams(vmem_limit_bytes=24 * MIB),
        cost_estimate=pl.CostEstimate(flops=8 * rows * depth * 384, bytes_accessed=5 * MIB, transcendentals=0),
    )(spot, *parts, *extra)


def attend_kernel(counts, spot_ref, *refs):
    kv_refs, q_refs = refs[: len(counts)], refs[len(counts) : len(counts) + 4]
    *out_refs, q_cat, k_cat, v_cat, e_ref, sd_ref, held_ref = refs[len(counts) + 4 :]
    rows = 128
    for i, ref in enumerate(q_refs):
        q_cat[i * rows : (i + 1) * rows, :128] = ref[1]
        q_cat[i * rows : (i + 1) * rows, 128:] = ref[0]
    at = 0
    for count, ref in zip(counts, kv_refs):
        for n in range(count):
            k_cat[at : at + rows, :128] = ref[4 * n]
            k_cat[at : at + rows, 128:] = ref[4 * n + 1]
            v_cat[at : at + rows, :128] = ref[4 * n + 2]
            v_cat[at : at + rows, 128:] = ref[4 * n + 3]
            at += rows
    inverse = 128.0 ** -0.5
    chunk = 256
    total_rows = q_cat.shape[0]
    weight_sum = jnp.zeros((total_rows, 128), f32)
    dot_sum = jnp.zeros((total_rows, 128), f32)
    for at in range(0, k_cat.shape[0], chunk):
        keys = k_cat[at : at + chunk, :]
        scores = dot_nt(q_cat[:, 128:], keys[:, :128])
        scores_dot = dot_nt(q_cat[...], keys)
        weights = jnp.exp2(scores * (inverse * 1.4426950408889634))
        e_ref[:, at : at + chunk] = weights
        sd_ref[:, at : at + chunk] = scores_dot
        both = weights * scores_dot
        weight_sum += weights[:, :128] + weights[:, 128:]
        dot_sum += both[:, :128] + both[:, 128:]
    scale = 1.0 / jnp.sum(weight_sum, axis=-1, keepdims=True)
    center = jnp.sum(dot_sum, axis=-1, keepdims=True) * scale
    summed = jnp.zeros((total_rows, 256), f32)
    summed_dot = jnp.zeros((total_rows, 128), f32)
    for at in range(0, k_cat.shape[0], chunk):
        weights = e_ref[:, at : at + chunk]
        weights_dot = (weights * (sd_ref[:, at : at + chunk] - center)).astype(bf16)
        values = v_cat[at : at + chunk, :]
        summed += jnp.dot(weights.astype(bf16), values, preferred_element_type=f32)
        summed_dot += jnp.dot(weights_dot, values[:, :128], preferred_element_type=f32)
    primal = (summed[:, :128] * scale).astype(bf16)
    tangent = ((summed[:, 128:] + summed_dot * inverse) * scale).astype(bf16)
    for i in range(4):
        held_ref[i, :rows] = primal[i * rows : (i + 1) * rows]
        held_ref[i, rows:] = tangent[i * rows : (i + 1) * rows]
    for i, ref in enumerate(out_refs):
        ref[...] = held_ref[spot_ref[i]]


def attend(spot, key_parts, query_parts):
    counts = tuple(part.shape[0] // 4 for part in key_parts)
    keys = 128 * sum(counts)
    return pl.pallas_call(
        functools.partial(attend_kernel, counts),
        in_specs=[smem] + [vmem] * (len(counts) + 4),
        out_specs=[vmem] * 4,
        out_shape=[jax.ShapeDtypeStruct((256, 128), bf16)] * 4,
        scratch_shapes=[
            pltpu.VMEM((512, 256), bf16),
            pltpu.VMEM((keys, 256), bf16),
            pltpu.VMEM((keys, 256), bf16),
            pltpu.VMEM((512, keys), f32),
            pltpu.VMEM((512, keys), f32),
            pltpu.VMEM((4, 256, 128), bf16),
        ],
        compiler_params=pltpu.CompilerParams(vmem_limit_bytes=24 * MIB),
        cost_estimate=pl.CostEstimate(
            flops=2 * 512 * keys * 128 * 6, bytes_accessed=3 * MIB, transcendentals=512 * keys
        ),
    )(spot, *key_parts, *query_parts)


def finish_kernel(place_ref, h0, h1, h2, h3, own_ref, other_ref, tok_ref, tan_ref, gate_ref, out_ref, out_dot_ref):
    rows = tok_ref.shape[0]
    y, zh, c = (place_ref[i] for i in range(3))
    total = None
    for m, ref in enumerate((h0, h1, h2, h3)):
        for first, w_ref in ((2 * c, own_ref), (2 - 2 * c, other_ref)):
            left = jnp.concatenate([ref[(zh - first + 4) % 4], ref[(zh - first + 3) % 4]], axis=1)
            term = dot_nt(left, w_ref[(y + m) % 4].reshape(-1, left.shape[1]))
            total = term if total is None else total + term
    gate = gate_ref[...]
    out_ref[...] = (tok_ref[...].astype(f32) + gate * total[:rows]).astype(bf16)
    out_dot_ref[...] = (tan_ref[...].astype(f32) + gate * total[rows:]).astype(bf16)


def finish(place, parts, own, other, tokens, tangents, gate):
    rows, cols = tokens.shape
    return pl.pallas_call(
        finish_kernel,
        in_specs=[smem] + [vmem] * 9,
        out_specs=[vmem] * 2,
        out_shape=[jax.ShapeDtypeStruct((rows, cols), bf16)] * 2,
        compiler_params=pltpu.CompilerParams(vmem_limit_bytes=24 * MIB),
        cost_estimate=pl.CostEstimate(flops=4 * rows * cols * 2048, bytes_accessed=6 * MIB, transcendentals=0),
    )(place, *parts, own, other, tokens, tangents, gate)


def from_ahead(array, axis, k):
    if k % 4 == 0:
        return array
    return lax.ppermute(array, axis, [(i, (i - k) % 4) for i in range(4)])


def swap(array, axis):
    return lax.ppermute(array, axis, [(0, 1), (1, 0)])


def beside(array, axis, sign):
    perm = [(2 * i + core, 2 * ((i - sign * (1 - 2 * core)) % 4) + core) for i in range(4) for core in range(2)]
    return lax.ppermute(array, (axis, "c"), perm)


def pick(array, index, axis=0):
    return lax.dynamic_index_in_dim(array, index, axis, keepdims=False)


def place(pieces, positions):
    out = jnp.zeros((len(pieces),) + pieces[0].shape, pieces[0].dtype)
    for piece, position in zip(pieces, positions):
        out = lax.dynamic_update_index_in_dim(out, piece, position, 0)
    return out


def after(array, *others):
    return lax.optimization_barrier((array,) + others)[0]


def per_device(tokens, tangents, qkv_weight, out_weight, mod_shift, mod_scale, mod_gate, query_gain, key_gain):
    zh, x, y = (lax.axis_index(name) for name in ("zh", "x", "y"))
    zl, c = lax.axis_index("zl"), lax.axis_index("c")
    clip = 2 * zl + c
    rows, features = tokens.shape
    share = features // 4
    ahead = lambda base, k: (base + k) % 4

    side = 1 - 2 * c
    ring = lambda base: [base, (base + side) % 4, (base + 2) % 4, (base - side) % 4]

    normed, quarter = modulate(y, tokens, tangents, mod_shift, mod_scale)
    normed = normed.reshape(4, 2 * rows, share)
    own_weight = pick(qkv_weight, clip, 1).reshape(qkv_weight.shape[0], 384)
    half = lax.dynamic_slice_in_dim(out_weight, 2 * c, 2, 1).reshape(-1, 256)
    near = swap(normed, "c")
    quarter = swap(quarter.reshape(2 * rows, share), "zl")
    near, quarter, own_weight = lax.optimization_barrier((near, quarter, own_weight))

    far_own = lax.all_gather(quarter, "y")
    columns = place([from_ahead(own_weight, "zh", k) for k in range(4)], [ahead(zh, k) for k in range(4)])
    columns = columns.reshape(-1, 384)
    up, down = beside(columns, "x", 1), beside(columns, "x", -1)
    half = after(half, columns)
    half = lax.ppermute(half, ("zh", "y"), [(a * 4 + b, b * 4 + a) for a in range(4) for b in range(4)])
    up, down, half = lax.optimization_barrier((up, down, half))
    opposite = beside(up, "x", 1)
    far_other = swap(after(far_own, up, down), "c")

    spot = jnp.stack([x, (side + 4) % 4]).astype(jnp.int32)
    three = [columns, up, down]
    near_total = project_three(spot, [normed, near], three)
    far_total = project_three(spot, [far_own, far_other], three)
    gains = jnp.stack([query_gain, key_gain])
    spot = jnp.stack([ahead(x, 2)] + [ahead(zh, k) ^ clip for k in range(4)]).astype(jnp.int32)
    first, *blocks = project_last(
        spot, [normed, near, far_own, far_other], opposite, near_total, far_total, gains
    )

    half_rows = lax.all_gather(half, ("zh", "x"))

    def along_x(group):
        return [from_ahead(group, "x", m) for m in range(1, 4)]

    queries = {k: blocks[3 + k] for k in range(4)}
    got = {k: from_ahead(blocks[k - 1], "zh", -k) for k in (1, 3)}
    second = along_x(first)
    got[1], got[3], *second = lax.optimization_barrier((got[1], got[3], *second))
    got[2] = from_ahead(after(blocks[1], got[1], got[3], *second), "zh", -2)
    third = along_x(jnp.concatenate([got[1], got[3]]))
    queries[1] = from_ahead(after(queries[1], got[1], got[3]), "zh", -1)
    got[2], third[0] = lax.optimization_barrier((got[2], third[0]))
    fourth = along_x(got[2])
    queries[2] = from_ahead(after(queries[2], got[2]), "zh", -2)
    queries[3] = from_ahead(after(queries[3], got[2]), "zh", -3)
    spot = jnp.stack([ahead(zh, -clip - i) for i in range(4)]).astype(jnp.int32)
    key_parts = [first, got[1], got[2], got[3], *second, *third, *fourth]
    attended = attend(spot, key_parts, [queries[k] for k in range(4)])

    heads = []
    for i in range(4):
        perm = [(a * 4 + j, ((j + i) % 4) * 4 + a) for a in range(4) for j in range(4)]
        heads.append(lax.ppermute(attended[i], ("zh", "zl", "c"), perm))
    heads = jnp.stack(heads)
    all_heads = [from_ahead(heads, "y", m) for m in range(4)]
    own = half_rows.reshape(4, 4, -1, 256)
    other = swap(after(own, heads), "c")

    offset = y * share
    tokens_part = lax.dynamic_slice_in_dim(tokens, offset, share, 1)
    tangents_part = lax.dynamic_slice_in_dim(tangents, offset, share, 1)
    gate_part = lax.dynamic_slice_in_dim(mod_gate, offset, share, 0).reshape(1, share)
    spot = jnp.stack([y, zh, c]).astype(jnp.int32)
    result, result_tangent = finish(spot, all_heads, own, other, tokens_part, tangents_part, gate_part)
    return (result, result_tangent)


def solution(mesh):
    split = Mesh(mesh.devices.reshape(4, 4, 4, 2, 2), ("zh", "x", "y", "zl", "c"))
    rows = P(("zl", "c", "zh", "x"), None)
    clip = P(("zl", "c"))
    return jax.shard_map(
        per_device,
        mesh=split,
        in_specs=(
            rows,
            rows,
            P(("zh", "x"), "y", None, None),
            P(("zh", "x"), "y", None),
            clip,
            clip,
            clip,
            P(),
            P(),
        ),
        out_specs=(P(("zl", "c", "zh", "x"), "y"), P(("zl", "c", "zh", "x"), "y")),
        check_vma=False,
    )
```
